32 devices in a mesh: gr: 4 (over y, x), gc: 8 (over z, core).
Axes of the slice: x: 2, y: 2, z: 4, core: 2. Of those that a mesh axis runs over, the one named last changes fastest.
Arguments:
- samples: bfloat16 [1024, 16384], P(('gr', 'gc')), may hold values from -6 to 6
- ridge: float32 [16384], replicated, may hold values from 1 to 4
Outputs:
- factored: float32 [4, 32, 128, 8, 16, 128], P('gr', None, None, 'gc')
The draws below stay inside these ranges and needn't reach their ends.
All inputs are finite; a program needn't handle non-finite values.
Results may differ from the reference program's by a relative error of at most 0.0003.
Values may be sent and summed in bfloat16 or wider, within the bound.
A program may use at most 128 MiB of HBM per device.

```python
import math
import jax
import jax.numpy as jnp
from jax import lax

D = 16384
B = 128
P_SIZE = 512
NS = 1024
TR = 32
TC = 16
N_GR = 4
N_GC = 8


def block_scale(rng, dims, split, least, largest):
    loudness = 1.0
    for position, shards_of in split:
        draws = jax.random.uniform(jax.random.fold_in(jax.random.fold_in(rng, 6), position), (shards_of,), jnp.float32, least / len(split), largest / len(split))
        loudness = loudness * jnp.repeat(jnp.exp(draws), dims[position] // shards_of).reshape((-1,) + (1,) * (len(dims) - 1 - position))
    return loudness


def noise(own_key, dims, spread, bound, pieces=(), kind=jnp.bfloat16):
    drawn = jax.random.normal(own_key, dims, jnp.float32) * spread
    if len(pieces) > 0:
        drawn = block_scale(own_key, dims, pieces, -0.22, 0.18) * drawn
    return jnp.clip(drawn, min=-bound, max=bound).astype(kind)


def setup_inputs(seed: int = 0) -> dict:
    seeds = jax.random.split(jax.random.key(seed), 3)
    return {
        "samples": noise(seeds[0], (NS, D), 1.0, 6.0, ((0, 32),)),
        "ridge": jnp.clip(jnp.exp(jax.random.uniform(seeds[1], (D,), jnp.float32, math.log(1.0), math.log(4.0))), 1.0, 4.0),
    }


def reference(samples, ridge):
    count = samples.shape[0]
    cov = jnp.dot(samples.T.astype(jnp.float32), samples.astype(jnp.float32), preferred_element_type=jnp.float32) / count
    where_diag = jnp.arange(D)
    cov = cov.at[where_diag, where_diag].add(ridge)
    corner = cov[:P_SIZE, :P_SIZE]
    lower = jnp.linalg.cholesky(corner)
    inverse = jax.scipy.linalg.solve_triangular(lower, jnp.eye(P_SIZE, dtype=jnp.float32), lower=True)
    panel = jnp.dot(cov[:, :P_SIZE].astype(jnp.float32), inverse.T.astype(jnp.float32), precision=lax.Precision.HIGHEST, preferred_element_type=jnp.float32)
    trail = cov[P_SIZE:, P_SIZE:] - jnp.dot(panel[P_SIZE:].astype(jnp.float32), panel[P_SIZE:].T.astype(jnp.float32), precision=lax.Precision.HIGHEST, preferred_element_type=jnp.float32)
    cov = cov.at[P_SIZE:, P_SIZE:].set(trail)
    cov = cov.at[:, :P_SIZE].set(panel)
    return cov.reshape(TR, N_GR, B, TC, N_GC, B).transpose(1, 0, 2, 4, 3, 5)
```

```python
import functools

import jax
import jax.numpy as jnp
from jax import lax
from jax.experimental import pallas as pl
from jax.experimental.pallas import tpu as pltpu
from jax.sharding import PartitionSpec as P

B = 128
P_SIZE = 512
TILES = P_SIZE // B
MIB = 1 << 20
EXACT = lax.Precision.HIGHEST
F32 = jnp.float32
BF16 = jnp.bfloat16


def dot(left, right, dims, precision=None):
    return lax.dot_general(
        left, right, ((dims[:1], dims[1:]), ((), ())), precision=precision,
        preferred_element_type=F32,
    )


def halves(value):
    high = value.astype(BF16)
    return high, (value - high.astype(F32)).astype(BF16)


def eye(n):
    return lax.broadcasted_iota(jnp.int32, (n, n), 0) == lax.broadcasted_iota(
        jnp.int32, (n, n), 1
    )


def factor_block(block):
    rows = lax.broadcasted_iota(jnp.int32, (B, 1), 0)
    upper = block
    inverse = jnp.where(eye(B), 1.0, 0.0).astype(F32)
    for k in range(B):
        scale = lax.rsqrt(upper[k : k + 1, k : k + 1])
        column = jnp.where(rows > k, upper[:, k : k + 1] * scale, 0.0)
        top = upper[k : k + 1, :] * scale
        side = inverse[k : k + 1, :] * scale
        here = rows == k
        upper = jnp.where(here, top, upper - column * top)
        inverse = jnp.where(here, side, inverse - column * side)
    return upper, inverse


def factor_all(s0, ridge0, a_ref, lower_ref, inv_ref):
    total = s0.shape[0]
    diag = eye(P_SIZE)
    a_ref[...] = dot(s0, s0, (0, 0)) * (1.0 / total) + jnp.where(diag, ridge0, 0.0)
    inv_ref[...] = jnp.where(diag, 1.0, 0.0).astype(F32)
    row = lax.broadcasted_iota(jnp.int32, (P_SIZE, 1), 0)
    tri = lax.broadcasted_iota(jnp.int32, (B, B), 0) <= lax.broadcasted_iota(
        jnp.int32, (B, B), 1
    )

    def step(k, carry):
        at = pl.ds(pl.multiple_of(k * B, B), B)
        upper, inverse = factor_block(a_ref[at, at])
        upper = jnp.where(tri, upper, 0.0)
        below = dot(a_ref[:, at], inverse, (1, 1), EXACT)
        below = jnp.where(row >= (k + 1) * B, below, 0.0)
        lower_ref[:, at] = below
        lower_ref[at, at] = upper.T
        a_ref[...] -= dot(below, below, (1, 1), EXACT)
        side = dot(inverse, inv_ref[at, :], (1, 0), EXACT)
        inv_ref[...] -= dot(below, side, (1, 0), EXACT)
        inv_ref[at, :] = side
        return carry

    lax.fori_loop(0, TILES, step, 0)


def factor_kernel(s0_ref, ridge_ref, lower_ref, inv_ref, vh_ref, vl_ref, a_ref):
    s0 = s0_ref[...]
    total = s0.shape[0]
    factor_all(s0, ridge_ref[...], a_ref, lower_ref, inv_ref)
    inv = inv_ref[...]
    ainv = dot(inv, inv, (0, 0), EXACT) * (1.0 / total / total)
    high, low = halves(ainv)
    v = dot(s0, high, (1, 0)) + dot(s0, low, (1, 0))
    vh_ref[...], vl_ref[...] = halves(v)


def factor(s0, ridge0):
    total = s0.shape[0]
    square = jax.ShapeDtypeStruct((P_SIZE, P_SIZE), F32)
    tall = jax.ShapeDtypeStruct((total, P_SIZE), BF16)
    return pl.pallas_call(
        factor_kernel,
        out_shape=(square, square, tall, tall),
        scratch_shapes=[pltpu.VMEM((P_SIZE, P_SIZE), F32)],
        compiler_params=pltpu.CompilerParams(vmem_limit_bytes=48 * MIB),
        name="factor",
    )(s0, ridge0)


def weights_kernel(ids, s0_ref, sc_ref, vh_ref, vl_ref, lower_ref, inv_ref,
                   th_ref, tl_ref, strip_ref):
    total = s0_ref.shape[0]
    s0 = s0_ref[...]
    sc = sc_ref[...]
    h = dot(s0, sc, (0, 0))
    hh, hl = halves(h)
    vh = vh_ref[...]
    t = sc.astype(F32) * (1.0 / total) - (
        dot(vh, hh, (1, 0)) + dot(vh, hl, (1, 0)) + dot(vl_ref[...], hh, (1, 0))
    )
    th_ref[...], tl_ref[...] = halves(t)
    row_tile = jnp.minimum(ids[0], TILES - 1)
    col_tile = jnp.minimum(ids[1], TILES - 1)
    at_row = pl.ds(pl.multiple_of(row_tile * B, B), B)
    at_col = pl.ds(pl.multiple_of(col_tile * B, B), B)
    low_id, high_id = ids[0] * 0, ids[0]
    hrow = dot(s0_ref[:, at_row], sc, (0, 0))
    strip_ref[...] = hrow * (1.0 / total)

    @pl.when((pl.program_id(0) == 0) & (ids[1] < TILES))
    def _():
        strip_ref[:, :B] = lower_ref[at_row, at_col]
        high, low = halves(inv_ref[at_col, :])
        tp = (dot(s0, high, (1, 1)) + dot(s0, low, (1, 1))) * (1.0 / total)
        th_ref[:, :B], tl_ref[:, :B] = halves(tp)


def weights(ids, s0, sc, vh, vl, lower, inv):
    total, width = sc.shape
    bn = 256

    def whole(a):
        return pl.BlockSpec(a.shape, lambda j, ids: (0, 0))

    column = pl.BlockSpec((total, bn), lambda j, ids: (0, j))
    return pl.pallas_call(
        weights_kernel,
        out_shape=(
            jax.ShapeDtypeStruct((total, width), BF16),
            jax.ShapeDtypeStruct((total, width), BF16),
            jax.ShapeDtypeStruct((B, width), F32),
        ),
        grid_spec=pltpu.PrefetchScalarGridSpec(
            num_scalar_prefetch=1,
            grid=(width // bn,),
            in_specs=[whole(s0), column, whole(vh), whole(vl), whole(lower), whole(inv)],
            out_specs=[column, column, pl.BlockSpec((B, bn), lambda j, ids: (0, j))],
        ),
        compiler_params=pltpu.CompilerParams(vmem_limit_bytes=56 * MIB),
        name="weights",
    )(ids, s0, sc, vh, vl, lower, inv)


def outer_kernel(n_rows, n_cols, ids, sr_ref, th_ref, tl_ref, strip_ref, ridge_ref, out_ref):
    i0 = pl.program_id(0)
    bm = sr_ref.shape[1]
    width = th_ref.shape[1]
    tile_cols = width // B
    left = sr_ref[...].T
    bn = min(256, width)
    for n in range(width // bn):
        at = slice(n * bn, (n + 1) * bn)
        acc = dot(left, th_ref[:, at], (1, 0)) + dot(left, tl_ref[:, at], (1, 0))
        for q in range(bn // B):
            j = n * (bn // B) + q
            out_ref[pl.ds(j, bm, stride=tile_cols), :] = acc[:, q * B : (q + 1) * B]

    row_id, col_id = ids[0], ids[1]

    @pl.when((i0 == 0) & (row_id < TILES))
    def _():
        for j in range(tile_cols):
            out_ref[pl.ds(j, B, stride=tile_cols), :] = strip_ref[:, j * B : (j + 1) * B]

    for u in range(bm // B):
        t = (i0 * (bm // B) + u) * n_rows + row_id

        @pl.when((t >= TILES) & (lax.rem(t, n_cols) == col_id))
        def _():
            at = pl.ds(u * B * tile_cols + lax.div(t, n_cols), B, stride=tile_cols)
            out_ref[at, :] += jnp.where(eye(B), ridge_ref[pl.ds(t, 1), :], 0.0)


def outer(ids, sr, th, tl, strip, ridge, n_rows, n_cols):
    total, height = sr.shape
    width = th.shape[1]
    tile_cols = width // B
    bm = 512 if total <= 1024 else 256

    def whole(a):
        return pl.BlockSpec(a.shape, lambda i, ids: (0, 0), pipeline_mode=pl.Buffered(1))

    return pl.pallas_call(
        functools.partial(outer_kernel, n_rows, n_cols),
        out_shape=jax.ShapeDtypeStruct((height * tile_cols, B), F32),
        grid_spec=pltpu.PrefetchScalarGridSpec(
            num_scalar_prefetch=1,
            grid=(height // bm,),
            in_specs=[
                pl.BlockSpec((total, bm), lambda i, ids: (0, i)),
                whole(th), whole(tl), whole(strip), whole(ridge),
            ],
            out_specs=pl.BlockSpec((bm * tile_cols, B), lambda i, ids: (i, 0)),
        ),
        compiler_params=pltpu.CompilerParams(vmem_limit_bytes=56 * MIB),
        name="outer",
    )(ids, sr, th, tl, strip, ridge)


def body(samples, ridge):
    row_id = lax.axis_index("gr")
    col_id = lax.axis_index("gc")
    n_rows = lax.axis_size("gr")
    n_cols = lax.axis_size("gc")
    per_dev, width = samples.shape
    tile_rows = width // (B * n_rows)
    tile_cols = width // (B * n_cols)
    row_slab = lax.all_to_all(
        samples.reshape(per_dev, tile_rows, n_rows, B),
        "gr",
        split_axis=2,
        concat_axis=0,
        tiled=True,
    ).reshape(n_rows * per_dev, tile_rows * B)
    col_slab = lax.all_to_all(
        samples.reshape(per_dev, tile_cols, n_cols, B),
        "gc",
        split_axis=2,
        concat_axis=0,
        tiled=True,
    ).reshape(n_cols * per_dev, tile_cols * B)
    first = lax.all_gather(
        lax.all_gather(samples[:, :P_SIZE], "gc", axis=0), "gr", axis=0
    ).reshape(-1, P_SIZE)
    cols_all = lax.all_gather(col_slab, "gr", axis=0, tiled=True)
    rows_all = (
        lax.all_gather(row_slab, "gc", axis=0)
        .reshape(n_cols, n_rows, per_dev, tile_rows * B)
        .transpose(1, 0, 2, 3)
        .reshape(-1, tile_rows * B)
    )
    ids = jnp.stack([row_id, col_id]).astype(jnp.int32)
    lower, inv, vh, vl = factor(first, ridge[:P_SIZE].reshape(1, P_SIZE))
    th, tl, strip = weights(ids, first, cols_all, vh, vl, lower, inv)
    result = outer(ids, rows_all, th, tl, strip, ridge.reshape(-1, B), n_rows, n_cols)
    return result.reshape(1, tile_rows, B, 1, tile_cols, B)


def solution(mesh):
    in_specs = (P(("gr", "gc"), None), P())
    out_specs = P("gr", None, None, "gc", None, None)
    return jax.shard_map(body, mesh=mesh, in_specs=in_specs, out_specs=out_specs, check_vma=False)
```

```python
import functools

import jax
import jax.numpy as jnp
from jax import lax
from jax.experimental import pallas as pl
from jax.experimental.pallas import tpu as pltpu
from jax.sharding import PartitionSpec as P

B = 128
P_SIZE = 512
TILES = P_SIZE // B
MIB = 1 << 20
EXACT = lax.Precision.HIGHEST
F32 = jnp.float32
BF16 = jnp.bfloat16


def dot(left, right, dims, precision=None):
    return lax.dot_general(
        left, right, ((dims[:1], dims[1:]), ((), ())), precision=precision,
        preferred_element_type=F32,
    )


def halves(value):
    high = value.astype(BF16)
    return high, (value - high.astype(F32)).astype(BF16)


def eye(n):
    return lax.broadcasted_iota(jnp.int32, (n, n), 0) == lax.broadcasted_iota(
        jnp.int32, (n, n), 1
    )


def factor_block(block):
    rows = lax.broadcasted_iota(jnp.int32, (B, 1), 0)
    upper = block
    inverse = jnp.where(eye(B), 1.0, 0.0).astype(F32)
    for k in range(B):
        scale = lax.rsqrt(upper[k : k + 1, k : k + 1])
        column = jnp.where(rows > k, upper[:, k : k + 1] * scale, 0.0)
        top = upper[k : k + 1, :] * scale
        side = inverse[k : k + 1, :] * scale
        here = rows == k
        upper = jnp.where(here, top, upper - column * top)
        inverse = jnp.where(here, side, inverse - column * side)
    return upper, inverse


def factor_start(s0, ridge0, a_ref, inv_ref):
    total = s0.shape[0]
    diag = eye(P_SIZE)
    a_ref[...] = dot(s0, s0, (0, 0)) * (1.0 / total) + jnp.where(diag, ridge0, 0.0)
    inv_ref[...] = jnp.where(diag, 1.0, 0.0).astype(F32)


def factor_step(k, a_ref, lower_ref, inv_ref):
    row = lax.broadcasted_iota(jnp.int32, (P_SIZE, 1), 0)
    tri = lax.broadcasted_iota(jnp.int32, (B, B), 0) <= lax.broadcasted_iota(
        jnp.int32, (B, B), 1
    )
    at = pl.ds(pl.multiple_of(k * B, B), B)
    upper, inverse = factor_block(a_ref[at, at])
    upper = jnp.where(tri, upper, 0.0)
    below = dot(a_ref[:, at], inverse, (1, 1), EXACT)
    below = jnp.where(row >= (k + 1) * B, below, 0.0)
    lower_ref[:, at] = below
    lower_ref[at, at] = upper.T
    a_ref[...] -= dot(below, below, (1, 1), EXACT)
    side = dot(inverse, inv_ref[at, :], (1, 0), EXACT)
    inv_ref[...] -= dot(below, side, (1, 0), EXACT)
    inv_ref[at, :] = side


def factor_end(s0, inv_ref, vh_ref, vl_ref):
    total = s0.shape[0]
    inv = inv_ref[...]
    ainv = dot(inv, inv, (0, 0), EXACT) * (1.0 / total / total)
    high, low = halves(ainv)
    v = dot(s0, high, (1, 0)) + dot(s0, low, (1, 0))
    vh_ref[...], vl_ref[...] = halves(v)


def gather_kernel(
    n_rows, n_cols, first_in, row_in, col_in, ridge_ref,
    rows, cols, first, lower_ref, inv_ref, vh_ref, vl_ref,
    a_ref, s0_ref, own_sem, load_sem,
    fp_s, fp_r, rp_s, rp_r, cz_s, cz_r, fz_s, fz_r, fx_s, fx_r,
    up_s, up_r, dn_s, dn_r, rx_s, rx_r, cp_s, cp_r,
):
    g = lax.axis_index("gr")
    c = lax.axis_index("gc")
    line = n_cols // 2
    place = c // 2
    core = c % 2
    pair = c + 1 - 2 * core

    def push(src, dst, send, recv, to_g, to_c):
        return pltpu.make_async_remote_copy(
            src_ref=src, dst_ref=dst, send_sem=send, recv_sem=recv,
            device_id=(to_g, to_c), device_id_type=pl.DeviceIdType.MESH,
        )

    barrier = pltpu.get_barrier_semaphore()
    for d in range(1, n_rows):
        pl.semaphore_signal(barrier, inc=1, device_id=((g + d) % n_rows, c),
                            device_id_type=pl.DeviceIdType.MESH)
    for d in range(1, n_cols):
        pl.semaphore_signal(barrier, inc=1, device_id=(g, (c + d) % n_cols),
                            device_id_type=pl.DeviceIdType.MESH)
    pl.semaphore_wait(barrier, n_rows + n_cols - 2)

    def first_plane(d):
        return push(first_in, first.at[c, g], fp_s.at[d], fp_r.at[d], (g + d) % n_rows, c)

    def row_plane(d):
        to = (g + d) % n_rows
        return push(row_in.at[to], rows.at[c, g], rp_s.at[d], rp_r.at[d], to, c)

    def col_line(d):
        to = (c + d) % n_cols
        return push(col_in.at[to], cols.at[c, g], cz_s.at[d], cz_r.at[d], g, to)

    def first_line(d):
        to = (place + d) % line * 2 + core
        return push(first.at[c], first.at[c], fz_s.at[d], fz_r.at[d], g, to)

    def first_pair(d):
        block = (place + d) % line * 2 + core
        return push(first.at[block], first.at[block], fx_s.at[d], fx_r.at[d], g, pair)

    def row_pair(block):
        at = block // 2
        return push(rows.at[block], rows.at[block], rx_s.at[at], rx_r.at[at], g, pair)

    def row_up(s):
        block = c - 2 * s
        return push(rows.at[block], rows.at[block], up_s.at[s], up_r.at[s], g, c + 2)

    def row_down(s):
        block = c + 2 * s
        return push(rows.at[block], rows.at[block], dn_s.at[s], dn_r.at[s], g, c - 2)

    def col_plane(d):
        return push(cols.at[:, g], cols.at[:, g], cp_s.at[d], cp_r.at[d], (g + d) % n_rows, c)

    def send_rows(s):
        @pl.when((place >= s) & (place + 1 < line))
        def _():
            row_up(s).start()

        @pl.when((place + s < line) & (place > 0))
        def _():
            row_down(s).start()

    def relay_rows(s):
        @pl.when(place > s)
        def _():
            row_up(s).wait_recv()
            row_pair(c - 2 * (s + 1)).start()

        @pl.when(place + s + 1 < line)
        def _():
            row_down(s).wait_recv()
            row_pair(c + 2 * (s + 1)).start()

        if s + 1 < line - 1:
            send_rows(s + 1)

    own = [
        pltpu.make_async_copy(first_in, first.at[c, g], own_sem.at[0]),
        pltpu.make_async_copy(row_in.at[g], rows.at[c, g], own_sem.at[1]),
        pltpu.make_async_copy(col_in.at[c], cols.at[c, g], own_sem.at[2]),
    ]
    for copy in own:
        copy.start()
    for d in range(1, n_rows):
        first_plane(d).start()
    for d in range(1, n_rows):
        row_plane(d).start()
    for copy in own:
        copy.wait()
    for d in range(1, n_rows):
        first_plane(d).wait_recv()
    for d in range(1, line):
        first_line(d).start()
    first_pair(0).start()
    for d in range(1, n_cols):
        col_line(d).start()
    for d in range(1, n_rows):
        row_plane(d).wait_recv()
    send_rows(0)
    row_pair(c).start()
    for d in range(1, line):
        first_line(d).wait_recv()
        first_pair(line - d).start()
    for d in range(line):
        first_pair(d).wait_recv()
    load = pltpu.make_async_copy(first, s0_ref, load_sem)
    load.start()
    load.wait()
    s0 = s0_ref[...].reshape(-1, P_SIZE)
    factor_start(s0, ridge_ref[...], a_ref, inv_ref)

    def col_gather():
        for d in range(1, n_cols):
            col_line(d).wait_recv()
        for d in range(1, n_rows):
            col_plane(d).start()

    def step(k, carry):
        factor_step(k, a_ref, lower_ref, inv_ref)

        @pl.when(k == 0)
        def _():
            col_gather()

        @pl.when(k == 1)
        def _():
            relay_rows(0)

        @pl.when(k == 3)
        def _():
            relay_rows(1)

        return carry

    lax.fori_loop(0, TILES, step, 0)
    factor_end(s0_ref[...].reshape(-1, P_SIZE), inv_ref, vh_ref, vl_ref)
    for s in range(2, line - 1):
        relay_rows(s)
    for d in range(1, n_rows):
        col_plane(d).wait_recv()
    for q in range(line):
        block = 2 * q + core
        row_pair(block).wait_recv()
    for d in range(1, n_rows):
        first_plane(d).wait_send()
        row_plane(d).wait_send()
        col_plane(d).wait_send()
    for d in range(1, n_cols):
        col_line(d).wait_send()
    for d in range(1, line):
        first_line(d).wait_send()
    for d in range(line):
        first_pair(d).wait_send()
        row_pair(2 * d + core).wait_send()
    for s in range(line - 1):
        @pl.when((place >= s) & (place + 1 < line))
        def _():
            row_up(s).wait_send()

        @pl.when((place + s < line) & (place > 0))
        def _():
            row_down(s).wait_send()


def gather(first_in, row_in, col_in, ridge0, n_rows, n_cols):
    per_dev = first_in.shape[0]
    total = per_dev * n_rows * n_cols
    square = jax.ShapeDtypeStruct((P_SIZE, P_SIZE), F32)
    tall = jax.ShapeDtypeStruct((total, P_SIZE), BF16)
    line = n_cols // 2

    def gathered(width):
        return jax.ShapeDtypeStruct((n_cols, n_rows, per_dev, width), BF16)

    far = pl.BlockSpec(memory_space=pl.ANY)
    near = pl.BlockSpec(memory_space=pltpu.VMEM)
    counts = [n_rows, n_rows, n_cols, line, line, line, line, line, n_rows]
    sems = [pltpu.SemaphoreType.DMA((n,)) for n in counts for _ in range(2)]
    return pl.pallas_call(
        functools.partial(gather_kernel, n_rows, n_cols),
        out_shape=(
            gathered(row_in.shape[2]), gathered(col_in.shape[2]), gathered(P_SIZE),
            square, square, tall, tall,
        ),
        in_specs=[far, far, far, near],
        out_specs=[far, far, far, near, near, near, near],
        scratch_shapes=[
            pltpu.VMEM((P_SIZE, P_SIZE), F32),
            pltpu.VMEM((n_cols, n_rows, per_dev, P_SIZE), BF16),
            pltpu.SemaphoreType.DMA((3,)),
            pltpu.SemaphoreType.DMA,
        ] + sems,
        compiler_params=pltpu.CompilerParams(
            vmem_limit_bytes=48 * MIB, collective_id=0, has_side_effects=True
        ),
        name="gather",
    )(first_in, row_in, col_in, ridge0)


def weights_kernel(ids, s0_ref, sc_ref, vh_ref, vl_ref, lower_ref, inv_ref,
                   th_ref, tl_ref, strip_ref):
    total = s0_ref.shape[0]
    s0 = s0_ref[...]
    sc = sc_ref[...]
    h = dot(s0, sc, (0, 0))
    hh, hl = halves(h)
    vh = vh_ref[...]
    t = sc.astype(F32) * (1.0 / total) - (
        dot(vh, hh, (1, 0)) + dot(vh, hl, (1, 0)) + dot(vl_ref[...], hh, (1, 0))
    )
    th_ref[...], tl_ref[...] = halves(t)
    row_tile = jnp.minimum(ids[0], TILES - 1)
    col_tile = jnp.minimum(ids[1], TILES - 1)
    at_row = pl.ds(pl.multiple_of(row_tile * B, B), B)
    at_col = pl.ds(pl.multiple_of(col_tile * B, B), B)
    hrow = dot(s0_ref[:, at_row], sc, (0, 0))
    strip_ref[...] = hrow * (1.0 / total)

    @pl.when((pl.program_id(0) == 0) & (ids[1] < TILES))
    def _():
        strip_ref[:, :B] = lower_ref[at_row, at_col]
        high, low = halves(inv_ref[at_col, :])
        tp = (dot(s0, high, (1, 1)) + dot(s0, low, (1, 1))) * (1.0 / total)
        th_ref[:, :B], tl_ref[:, :B] = halves(tp)


def weights(ids, s0, sc, vh, vl, lower, inv):
    total, width = sc.shape
    bn = 256

    def whole(a):
        return pl.BlockSpec(a.shape, lambda j, ids: (0, 0))

    column = pl.BlockSpec((total, bn), lambda j, ids: (0, j))
    return pl.pallas_call(
        weights_kernel,
        out_shape=(
            jax.ShapeDtypeStruct((total, width), BF16),
            jax.ShapeDtypeStruct((total, width), BF16),
            jax.ShapeDtypeStruct((B, width), F32),
        ),
        grid_spec=pltpu.PrefetchScalarGridSpec(
            num_scalar_prefetch=1,
            grid=(width // bn,),
            in_specs=[whole(s0), column, whole(vh), whole(vl), whole(lower), whole(inv)],
            out_specs=[column, column, pl.BlockSpec((B, bn), lambda j, ids: (0, j))],
        ),
        compiler_params=pltpu.CompilerParams(vmem_limit_bytes=56 * MIB),
        name="weights",
    )(ids, s0, sc, vh, vl, lower, inv)


def outer_kernel(n_rows, n_cols, ids, sr_ref, th_ref, tl_ref, strip_ref, ridge_ref, out_ref):
    i0 = pl.program_id(0)
    bm = sr_ref.shape[1]
    width = th_ref.shape[1]
    tile_cols = width // B
    left = sr_ref[...].T
    bn = min(256, width)
    for n in range(width // bn):
        at = slice(n * bn, (n + 1) * bn)
        acc = dot(left, th_ref[:, at], (1, 0)) + dot(left, tl_ref[:, at], (1, 0))
        for q in range(bn // B):
            j = n * (bn // B) + q
            out_ref[pl.ds(j, bm, stride=tile_cols), :] = acc[:, q * B : (q + 1) * B]

    row_id, col_id = ids[0], ids[1]

    @pl.when((i0 == 0) & (row_id < TILES))
    def _():
        for j in range(tile_cols):
            out_ref[pl.ds(j, B, stride=tile_cols), :] = strip_ref[:, j * B : (j + 1) * B]

    for u in range(bm // B):
        t = (i0 * (bm // B) + u) * n_rows + row_id

        @pl.when((t >= TILES) & (lax.rem(t, n_cols) == col_id))
        def _():
            at = pl.ds(u * B * tile_cols + lax.div(t, n_cols), B, stride=tile_cols)
            out_ref[at, :] += jnp.where(eye(B), ridge_ref[pl.ds(t, 1), :], 0.0)


def outer(ids, sr, th, tl, strip, ridge, n_rows, n_cols):
    total, height = sr.shape
    width = th.shape[1]
    tile_cols = width // B
    bm = 512 if total <= 1024 else 256

    def whole(a):
        return pl.BlockSpec(a.shape, lambda i, ids: (0, 0), pipeline_mode=pl.Buffered(1))

    return pl.pallas_call(
        functools.partial(outer_kernel, n_rows, n_cols),
        out_shape=jax.ShapeDtypeStruct((height * tile_cols, B), F32),
        grid_spec=pltpu.PrefetchScalarGridSpec(
            num_scalar_prefetch=1,
            grid=(height // bm,),
            in_specs=[
                pl.BlockSpec((total, bm), lambda i, ids: (0, i)),
                whole(th), whole(tl), whole(strip), whole(ridge),
            ],
            out_specs=pl.BlockSpec((bm * tile_cols, B), lambda i, ids: (i, 0)),
        ),
        compiler_params=pltpu.CompilerParams(vmem_limit_bytes=56 * MIB),
        name="outer",
    )(ids, sr, th, tl, strip, ridge)


def body(samples, ridge):
    row_id = lax.axis_index("gr")
    col_id = lax.axis_index("gc")
    n_rows = lax.axis_size("gr")
    n_cols = lax.axis_size("gc")
    per_dev, width = samples.shape
    tile_rows = width // (B * n_rows)
    tile_cols = width // (B * n_cols)
    row_in = samples.reshape(per_dev, tile_rows, n_rows, B).transpose(2, 0, 1, 3)
    col_in = samples.reshape(per_dev, tile_cols, n_cols, B).transpose(2, 0, 1, 3)
    rows_all, cols_all, first, lower, inv, vh, vl = gather(
        samples[:, :P_SIZE],
        row_in.reshape(n_rows, per_dev, -1),
        col_in.reshape(n_cols, per_dev, -1),
        ridge[:P_SIZE].reshape(1, P_SIZE),
        n_rows,
        n_cols,
    )
    total = per_dev * n_rows * n_cols
    rows_all = rows_all.reshape(total, -1)
    cols_all = cols_all.reshape(total, -1)
    first = first.reshape(total, -1)
    ids = jnp.stack([row_id, col_id]).astype(jnp.int32)
    th, tl, strip = weights(ids, first, cols_all, vh, vl, lower, inv)
    result = outer(ids, rows_all, th, tl, strip, ridge.reshape(-1, B), n_rows, n_cols)
    return result.reshape(1, tile_rows, B, 1, tile_cols, B)


def solution(mesh):
    in_specs = (P(("gr", "gc"), None), P())
    out_specs = P("gr", None, None, "gc", None, None)
    return jax.shard_map(body, mesh=mesh, in_specs=in_specs, out_specs=out_specs, check_vma=False)
```

```python
import functools

import jax
import jax.numpy as jnp
from jax import lax
from jax.experimental import pallas as pl
from jax.experimental.pallas import tpu as pltpu
from jax.sharding import PartitionSpec as P

B = 128
P_SIZE = 512
TILES = P_SIZE // B
MIB = 1 << 20
EXACT = lax.Precision.HIGHEST
F32 = jnp.float32
BF16 = jnp.bfloat16


def dot(left, right, dims, precision=None):
    return lax.dot_general(
        left, right, ((dims[:1], dims[1:]), ((), ())), precision=precision,
        preferred_element_type=F32,
    )


def halves(value):
    high = value.astype(BF16)
    return high, (value - high.astype(F32)).astype(BF16)


def eye(n):
    return lax.broadcasted_iota(jnp.int32, (n, n), 0) == lax.broadcasted_iota(
        jnp.int32, (n, n), 1
    )


def factor_block(block):
    rows = lax.broadcasted_iota(jnp.int32, (B, 1), 0)
    upper = block
    inverse = jnp.where(eye(B), 1.0, 0.0).astype(F32)
    for k in range(B):
        scale = lax.rsqrt(upper[k : k + 1, k : k + 1])
        column = jnp.where(rows > k, upper[:, k : k + 1] * scale, 0.0)
        top = upper[k : k + 1, :] * scale
        side = inverse[k : k + 1, :] * scale
        here = rows == k
        upper = jnp.where(here, top, upper - column * top)
        inverse = jnp.where(here, side, inverse - column * side)
    return upper, inverse


def factor_start(s0, ridge0, a_ref, inv_ref):
    total = s0.shape[0]
    diag = eye(P_SIZE)
    a_ref[...] = dot(s0, s0, (0, 0)) * (1.0 / total) + jnp.where(diag, ridge0, 0.0)
    inv_ref[...] = jnp.where(diag, 1.0, 0.0).astype(F32)


def factor_step(k, a_ref, lower_ref, inv_ref):
    row = lax.broadcasted_iota(jnp.int32, (P_SIZE, 1), 0)
    tri = lax.broadcasted_iota(jnp.int32, (B, B), 0) <= lax.broadcasted_iota(
        jnp.int32, (B, B), 1
    )
    at = pl.ds(pl.multiple_of(k * B, B), B)
    upper, inverse = factor_block(a_ref[at, at])
    upper = jnp.where(tri, upper, 0.0)
    below = dot(a_ref[:, at], inverse, (1, 1), EXACT)
    below = jnp.where(row >= (k + 1) * B, below, 0.0)
    lower_ref[:, at] = below
    lower_ref[at, at] = upper.T
    a_ref[...] -= dot(below, below, (1, 1), EXACT)
    side = dot(inverse, inv_ref[at, :], (1, 0), EXACT)
    inv_ref[...] -= dot(below, side, (1, 0), EXACT)
    inv_ref[at, :] = side


def factor_end(s0, inv_ref, vh_ref, vl_ref):
    total = s0.shape[0]
    inv = inv_ref[...]
    ainv = dot(inv, inv, (0, 0), EXACT) * (1.0 / total / total)
    high, low = halves(ainv)
    v = dot(s0, high, (1, 0)) + dot(s0, low, (1, 0))
    vh_ref[...], vl_ref[...] = halves(v)


def make_weights(g, c, s0_ref, sc_ref, vh_ref, vl_ref, lower_ref, inv_ref,
                 th_ref, tl_ref, strip_ref):
    total, width = th_ref.shape
    bn = min(256, width)
    row_tile = jnp.minimum(g, TILES - 1)
    col_tile = jnp.minimum(c, TILES - 1)
    at_row = pl.ds(pl.multiple_of(row_tile * B, B), B)
    at_col = pl.ds(pl.multiple_of(col_tile * B, B), B)

    def chunk(j, carry):
        at = pl.ds(pl.multiple_of(j * bn, bn), bn)
        s0 = s0_ref[...].reshape(-1, P_SIZE)
        sc = sc_ref[:, :, :, at].reshape(-1, bn)
        hh, hl = halves(dot(s0, sc, (0, 0)))
        vh = vh_ref[...]
        t = sc.astype(F32) * (1.0 / total) - (
            dot(vh, hh, (1, 0)) + dot(vh, hl, (1, 0)) + dot(vl_ref[...], hh, (1, 0))
        )
        th_ref[:, at], tl_ref[:, at] = halves(t)
        near = s0_ref[:, :, :, at_row].reshape(-1, B)
        strip_ref[:, at] = dot(near, sc, (0, 0)) * (1.0 / total)
        return carry

    lax.fori_loop(0, width // bn, chunk, 0)

    @pl.when(c < TILES)
    def _():
        strip_ref[:, :B] = lower_ref[at_row, at_col]
        high, low = halves(inv_ref[at_col, :])
        s0 = s0_ref[...].reshape(-1, P_SIZE)
        tp = (dot(s0, high, (1, 1)) + dot(s0, low, (1, 1))) * (1.0 / total)
        th_ref[:, :B], tl_ref[:, :B] = halves(tp)


def gather_kernel(
    n_rows, n_cols, first_in, row_in, col_in, ridge_ref,
    rows, cols, first, th_ref, tl_ref, strip_ref,
    a_ref, s0_ref, lower_ref, inv_ref, vh_ref, vl_ref, sc_ref, plane_ref, turned_ref,
    own_sem, load_sem,
    fp_s, fp_r, rp_s, rp_r, cz_s, cz_r, fz_s, fz_r, fx_s, fx_r,
    up_s, up_r, dn_s, dn_r, rx_s, rx_r, cp_s, cp_r,
):
    g = lax.axis_index("gr")
    c = lax.axis_index("gc")
    line = n_cols // 2
    place = c // 2
    core = c % 2
    pair = c + 1 - 2 * core

    def push(src, dst, send, recv, to_g, to_c):
        return pltpu.make_async_remote_copy(
            src_ref=src, dst_ref=dst, send_sem=send, recv_sem=recv,
            device_id=(to_g, to_c), device_id_type=pl.DeviceIdType.MESH,
        )

    barrier = pltpu.get_barrier_semaphore()
    for d in range(1, n_rows):
        pl.semaphore_signal(barrier, inc=1, device_id=((g + d) % n_rows, c),
                            device_id_type=pl.DeviceIdType.MESH)
    for d in range(1, n_cols):
        pl.semaphore_signal(barrier, inc=1, device_id=(g, (c + d) % n_cols),
                            device_id_type=pl.DeviceIdType.MESH)
    pl.semaphore_wait(barrier, n_rows + n_cols - 2)

    def first_plane(d):
        return push(first_in, first.at[c, g], fp_s.at[d], fp_r.at[d], (g + d) % n_rows, c)

    def row_plane(d):
        to = (g + d) % n_rows
        return push(row_in.at[to], plane_ref.at[g], rp_s.at[d], rp_r.at[d], to, c)

    def col_line(d):
        to = (c + d) % n_cols
        return push(col_in.at[to], cols.at[c, g], cz_s.at[d], cz_r.at[d], g, to)

    def first_line(d):
        to = (place + d) % line * 2 + core
        return push(first.at[c], first.at[c], fz_s.at[d], fz_r.at[d], g, to)

    def first_pair(d):
        block = (place + d) % line * 2 + core
        return push(first.at[block], first.at[block], fx_s.at[d], fx_r.at[d], g, pair)

    def row_pair(block):
        at = block // 2
        return push(rows.at[block], rows.at[block], rx_s.at[at], rx_r.at[at], g, pair)

    def row_up(s):
        block = c - 2 * s
        return push(rows.at[block], rows.at[block], up_s.at[s], up_r.at[s], g, c + 2)

    def row_down(s):
        block = c + 2 * s
        return push(rows.at[block], rows.at[block], dn_s.at[s], dn_r.at[s], g, c - 2)

    def col_plane(d):
        return push(cols.at[:, g], cols.at[:, g], cp_s.at[d], cp_r.at[d], (g + d) % n_rows, c)

    def send_rows(s):
        @pl.when((place >= s) & (place + 1 < line))
        def _():
            row_up(s).start()

        @pl.when((place + s < line) & (place > 0))
        def _():
            row_down(s).start()

    def relay_rows(s):
        @pl.when(place > s)
        def _():
            row_up(s).wait_recv()
            row_pair(c - 2 * (s + 1)).start()

        @pl.when(place + s + 1 < line)
        def _():
            row_down(s).wait_recv()
            row_pair(c + 2 * (s + 1)).start()

        if s + 1 < line - 1:
            send_rows(s + 1)

    own = [
        pltpu.make_async_copy(first_in, first.at[c, g], own_sem.at[0]),
        pltpu.make_async_copy(row_in.at[g], plane_ref.at[g], own_sem.at[1]),
        pltpu.make_async_copy(col_in.at[c], cols.at[c, g], own_sem.at[2]),
    ]
    for copy in own:
        copy.start()
    for d in range(1, n_rows):
        first_plane(d).start()
    for d in range(1, n_rows):
        row_plane(d).start()
    for copy in own:
        copy.wait()
    for d in range(1, n_rows):
        first_plane(d).wait_recv()
    for d in range(1, line):
        first_line(d).start()
    first_pair(0).start()
    for d in range(1, n_cols):
        col_line(d).start()
    for d in range(1, n_rows):
        row_plane(d).wait_recv()
    height = turned_ref.shape[0]
    for n in range(height // P_SIZE):
        at = slice(n * P_SIZE, (n + 1) * P_SIZE)
        turned_ref[at, :] = plane_ref[:, :, at].reshape(-1, P_SIZE).T
    turned = pltpu.make_async_copy(turned_ref, rows.at[c], own_sem.at[3])
    turned.start()
    turned.wait()
    send_rows(0)
    row_pair(c).start()
    for d in range(1, line):
        first_line(d).wait_recv()
        first_pair(line - d).start()
    for d in range(line):
        first_pair(d).wait_recv()
    load = pltpu.make_async_copy(first, s0_ref, load_sem)
    load.start()
    load.wait()
    s0 = s0_ref[...].reshape(-1, P_SIZE)
    factor_start(s0, ridge_ref[...], a_ref, inv_ref)

    def col_gather():
        for d in range(1, n_cols):
            col_line(d).wait_recv()
        for d in range(1, n_rows):
            col_plane(d).start()

    def step(k, carry):
        factor_step(k, a_ref, lower_ref, inv_ref)

        @pl.when(k == 0)
        def _():
            col_gather()

        @pl.when(k == 1)
        def _():
            relay_rows(0)

        @pl.when(k == 2)
        def _():
            relay_rows(1)

        return carry

    lax.fori_loop(0, TILES, step, 0)
    factor_end(s0_ref[...].reshape(-1, P_SIZE), inv_ref, vh_ref, vl_ref)
    for d in range(1, n_rows):
        col_plane(d).wait_recv()
    load = pltpu.make_async_copy(cols, sc_ref, load_sem)
    load.start()
    load.wait()
    make_weights(g, c, s0_ref, sc_ref, vh_ref, vl_ref, lower_ref, inv_ref,
                 th_ref, tl_ref, strip_ref)
    for s in range(2, line - 1):
        relay_rows(s)
    for q in range(line):
        block = 2 * q + core
        row_pair(block).wait_recv()
    for d in range(1, n_rows):
        first_plane(d).wait_send()
        row_plane(d).wait_send()
        col_plane(d).wait_send()
    for d in range(1, n_cols):
        col_line(d).wait_send()
    for d in range(1, line):
        first_line(d).wait_send()
    for d in range(line):
        first_pair(d).wait_send()
        row_pair(2 * d + core).wait_send()
    for s in range(line - 1):
        @pl.when((place >= s) & (place + 1 < line))
        def _():
            row_up(s).wait_send()

        @pl.when((place + s < line) & (place > 0))
        def _():
            row_down(s).wait_send()


def gather(first_in, row_in, col_in, ridge0, n_rows, n_cols):
    per_dev = first_in.shape[0]
    total = per_dev * n_rows * n_cols
    height, width = row_in.shape[2], col_in.shape[2]
    line = n_cols // 2

    def gathered(width):
        return jax.ShapeDtypeStruct((n_cols, n_rows, per_dev, width), BF16)

    far = pl.BlockSpec(memory_space=pl.ANY)
    near = pl.BlockSpec(memory_space=pltpu.VMEM)
    counts = [n_rows, n_rows, n_cols, line, line, line, line, line, n_rows]
    sems = [pltpu.SemaphoreType.DMA((n,)) for n in counts for _ in range(2)]
    return pl.pallas_call(
        functools.partial(gather_kernel, n_rows, n_cols),
        out_shape=(
            jax.ShapeDtypeStruct((n_cols, height, n_rows * per_dev), BF16),
            gathered(width), gathered(P_SIZE),
            jax.ShapeDtypeStruct((total, width), BF16),
            jax.ShapeDtypeStruct((total, width), BF16),
            jax.ShapeDtypeStruct((B, width), F32),
        ),
        in_specs=[far, far, far, near],
        out_specs=[far, far, far, near, near, near],
        scratch_shapes=[
            pltpu.VMEM((P_SIZE, P_SIZE), F32),
            pltpu.VMEM((n_cols, n_rows, per_dev, P_SIZE), BF16),
            pltpu.VMEM((P_SIZE, P_SIZE), F32),
            pltpu.VMEM((P_SIZE, P_SIZE), F32),
            pltpu.VMEM((total, P_SIZE), BF16),
            pltpu.VMEM((total, P_SIZE), BF16),
            pltpu.VMEM((n_cols, n_rows, per_dev, width), BF16),
            pltpu.VMEM((n_rows, per_dev, height), BF16),
            pltpu.VMEM((height, n_rows * per_dev), BF16),
            pltpu.SemaphoreType.DMA((4,)),
            pltpu.SemaphoreType.DMA,
        ] + sems,
        compiler_params=pltpu.CompilerParams(
            vmem_limit_bytes=58 * MIB, collective_id=0, has_side_effects=True
        ),
        name="gather",
    )(first_in, row_in, col_in, ridge0)


def outer_kernel(n_rows, n_cols, ids, sr_ref, th_ref, tl_ref, strip_ref, ridge_ref, out_ref):
    i0 = pl.program_id(0)
    bm = sr_ref.shape[1]
    blocks = sr_ref.shape[0]
    width = th_ref.shape[1]
    tile_cols = width // B
    left = jnp.concatenate([sr_ref[q] for q in range(blocks)], axis=1)
    bn = min(256, width)
    for n in range(width // bn):
        at = slice(n * bn, (n + 1) * bn)
        acc = dot(left, th_ref[:, at], (1, 0)) + dot(left, tl_ref[:, at], (1, 0))
        for q in range(bn // B):
            j = n * (bn // B) + q
            out_ref[pl.ds(j, bm, stride=tile_cols), :] = acc[:, q * B : (q + 1) * B]

    row_id, col_id = ids[0], ids[1]

    @pl.when((i0 == 0) & (row_id < TILES))
    def _():
        for j in range(tile_cols):
            out_ref[pl.ds(j, B, stride=tile_cols), :] = strip_ref[:, j * B : (j + 1) * B]

    for u in range(bm // B):
        t = (i0 * (bm // B) + u) * n_rows + row_id

        @pl.when((t >= TILES) & (lax.rem(t, n_cols) == col_id))
        def _():
            at = pl.ds(u * B * tile_cols + lax.div(t, n_cols), B, stride=tile_cols)
            out_ref[at, :] += jnp.where(eye(B), ridge_ref[pl.ds(t, 1), :], 0.0)


def outer(ids, sr, th, tl, strip, ridge, n_rows, n_cols):
    blocks, height, deep = sr.shape
    total = blocks * deep
    width = th.shape[1]
    tile_cols = width // B
    bm = 512 if total <= 1024 else 256

    def whole(a):
        return pl.BlockSpec(a.shape, lambda i, ids: (0, 0), pipeline_mode=pl.Buffered(1))

    return pl.pallas_call(
        functools.partial(outer_kernel, n_rows, n_cols),
        out_shape=jax.ShapeDtypeStruct((height * tile_cols, B), F32),
        grid_spec=pltpu.PrefetchScalarGridSpec(
            num_scalar_prefetch=1,
            grid=(height // bm,),
            in_specs=[
                pl.BlockSpec((blocks, bm, deep), lambda i, ids: (0, i, 0)),
                whole(th), whole(tl), whole(strip), whole(ridge),
            ],
            out_specs=pl.BlockSpec((bm * tile_cols, B), lambda i, ids: (i, 0)),
        ),
        compiler_params=pltpu.CompilerParams(vmem_limit_bytes=56 * MIB),
        name="outer",
    )(ids, sr, th, tl, strip, ridge)


def body(samples, ridge):
    row_id = lax.axis_index("gr")
    col_id = lax.axis_index("gc")
    n_rows = lax.axis_size("gr")
    n_cols = lax.axis_size("gc")
    per_dev, width = samples.shape
    tile_rows = width // (B * n_rows)
    tile_cols = width // (B * n_cols)
    row_in = samples.reshape(per_dev, tile_rows, n_rows, B).transpose(2, 0, 1, 3)
    col_in = samples.reshape(per_dev, tile_cols, n_cols, B).transpose(2, 0, 1, 3)
    rows_all, _, _, th, tl, strip = gather(
        samples[:, :P_SIZE],
        row_in.reshape(n_rows, per_dev, -1),
        col_in.reshape(n_cols, per_dev, -1),
        ridge[:P_SIZE].reshape(1, P_SIZE),
        n_rows,
        n_cols,
    )
    ids = jnp.stack([row_id, col_id]).astype(jnp.int32)
    result = outer(ids, rows_all, th, tl, strip, ridge.reshape(-1, B), n_rows, n_cols)
    return result.reshape(1, tile_rows, B, 1, tile_cols, B)


def solution(mesh):
    in_specs = (P(("gr", "gc"), None), P())
    out_specs = P("gr", None, None, "gc", None, None)
    return jax.shard_map(body, mesh=mesh, in_specs=in_specs, out_specs=out_specs, check_vma=False)
```

```python
import functools

import jax
import jax.numpy as jnp
from jax import lax
from jax.experimental import pallas as pl
from jax.experimental.pallas import tpu as pltpu
from jax.sharding import PartitionSpec as P

B = 128
P_SIZE = 512
TILES = P_SIZE // B
MIB = 1 << 20
EXACT = lax.Precision.HIGHEST
F32 = jnp.float32
BF16 = jnp.bfloat16
F8 = jnp.float8_e4m3fn
LOW_SCALE = float(1 << 19)


def dot(left, right, dims, precision=None):
    return lax.dot_general(
        left, right, ((dims[:1], dims[1:]), ((), ())), precision=precision,
        preferred_element_type=F32,
    )


def halves(value):
    high = value.astype(BF16)
    return high, (value - high.astype(F32)).astype(BF16)


def eye(n):
    return lax.broadcasted_iota(jnp.int32, (n, n), 0) == lax.broadcasted_iota(
        jnp.int32, (n, n), 1
    )


def factor_block(block):
    rows = lax.broadcasted_iota(jnp.int32, (B, 1), 0)
    upper = block
    inverse = jnp.where(eye(B), 1.0, 0.0).astype(F32)
    for k in range(B):
        scale = lax.rsqrt(upper[k : k + 1, k : k + 1])
        column = jnp.where(rows > k, upper[:, k : k + 1] * scale, 0.0)
        top = upper[k : k + 1, :] * scale
        side = inverse[k : k + 1, :] * scale
        here = rows == k
        upper = jnp.where(here, top, upper - column * top)
        inverse = jnp.where(here, side, inverse - column * side)
    return upper, inverse


def factor_start(s0, ridge0, a_ref, inv_ref):
    total = s0.shape[0]
    diag = eye(P_SIZE)
    a_ref[...] = dot(s0, s0, (0, 0)) * (1.0 / total) + jnp.where(diag, ridge0, 0.0)
    inv_ref[...] = jnp.where(diag, 1.0, 0.0).astype(F32)


def factor_step(k, a_ref, lower_ref, inv_ref):
    row = lax.broadcasted_iota(jnp.int32, (P_SIZE, 1), 0)
    tri = lax.broadcasted_iota(jnp.int32, (B, B), 0) <= lax.broadcasted_iota(
        jnp.int32, (B, B), 1
    )
    at = pl.ds(pl.multiple_of(k * B, B), B)
    upper, inverse = factor_block(a_ref[at, at])
    upper = jnp.where(tri, upper, 0.0)
    below = dot(a_ref[:, at], inverse, (1, 1), EXACT)
    below = jnp.where(row >= (k + 1) * B, below, 0.0)
    lower_ref[:, at] = below
    lower_ref[at, at] = upper.T
    a_ref[...] -= dot(below, below, (1, 1), EXACT)
    side = dot(inverse, inv_ref[at, :], (1, 0), EXACT)
    inv_ref[...] -= dot(below, side, (1, 0), EXACT)
    inv_ref[at, :] = side


def factor_end(s0, inv_ref, vh_ref, vl_ref):
    total = s0.shape[0]
    inv = inv_ref[...]
    ainv = dot(inv, inv, (0, 0), EXACT) * (1.0 / total / total)
    high, low = halves(ainv)
    v = dot(s0, high, (1, 0)) + dot(s0, low, (1, 0))
    vh_ref[...], vl_ref[...] = halves(v)


def make_weights(g, c, s0_ref, sc_ref, vh_ref, vl_ref, lower_ref, inv_ref,
                 th_ref, tl_ref, strip_ref):
    total, width = th_ref.shape
    bn = min(256, width)
    row_tile = jnp.minimum(g, TILES - 1)
    col_tile = jnp.minimum(c, TILES - 1)
    at_row = pl.ds(pl.multiple_of(row_tile * B, B), B)
    at_col = pl.ds(pl.multiple_of(col_tile * B, B), B)

    def chunk(j, carry):
        at = pl.ds(pl.multiple_of(j * bn, bn), bn)
        s0 = s0_ref[...].reshape(-1, P_SIZE)
        sc = sc_ref[:, :, :, at].reshape(-1, bn)
        hh, hl = halves(dot(s0, sc, (0, 0)))
        vh = vh_ref[...]
        t = sc.astype(F32) * (1.0 / total) - (
            dot(vh, hh, (1, 0)) + dot(vh, hl, (1, 0)) + dot(vl_ref[...], hh, (1, 0))
        )
        th_ref[:, at], tl_ref[:, at] = halves(t)
        near = s0_ref[:, :, :, at_row].reshape(-1, B)
        strip_ref[:, at] = dot(near, sc, (0, 0)) * (1.0 / total)
        return carry

    lax.fori_loop(0, width // bn, chunk, 0)

    @pl.when(c < TILES)
    def _():
        strip_ref[:, :B] = lower_ref[at_row, at_col]
        high, low = halves(inv_ref[at_col, :])
        s0 = s0_ref[...].reshape(-1, P_SIZE)
        tp = (dot(s0, high, (1, 1)) + dot(s0, low, (1, 1))) * (1.0 / total)
        th_ref[:, :B], tl_ref[:, :B] = halves(tp)


def gather_kernel(
    n_rows, n_cols, first_in, row_in, col_in, ridge_ref,
    rows, cols, first, th_ref, tl_ref, strip_ref,
    a_ref, s0_ref, lower_ref, inv_ref, vh_ref, vl_ref, sc_ref, plane_ref, turned_ref,
    own_sem, load_sem,
    fp_s, fp_r, rp_s, rp_r, cz_s, cz_r, fz_s, fz_r, fx_s, fx_r,
    up_s, up_r, dn_s, dn_r, rx_s, rx_r, cp_s, cp_r,
):
    g = lax.axis_index("gr")
    c = lax.axis_index("gc")
    line = n_cols // 2
    place = c // 2
    core = c % 2
    pair = c + 1 - 2 * core

    def push(src, dst, send, recv, to_g, to_c):
        return pltpu.make_async_remote_copy(
            src_ref=src, dst_ref=dst, send_sem=send, recv_sem=recv,
            device_id=(to_g, to_c), device_id_type=pl.DeviceIdType.MESH,
        )

    barrier = pltpu.get_barrier_semaphore()
    for d in range(1, n_rows):
        pl.semaphore_signal(barrier, inc=1, device_id=((g + d) % n_rows, c),
                            device_id_type=pl.DeviceIdType.MESH)
    for d in range(1, n_cols):
        pl.semaphore_signal(barrier, inc=1, device_id=(g, (c + d) % n_cols),
                            device_id_type=pl.DeviceIdType.MESH)
    pl.semaphore_wait(barrier, n_rows + n_cols - 2)

    def first_plane(d):
        return push(first_in, first.at[c, g], fp_s.at[d], fp_r.at[d], (g + d) % n_rows, c)

    def row_plane(d):
        to = (g + d) % n_rows
        return push(row_in.at[to], plane_ref.at[g], rp_s.at[d], rp_r.at[d], to, c)

    def col_line(d):
        to = (c + d) % n_cols
        return push(col_in.at[to], cols.at[c, g], cz_s.at[d], cz_r.at[d], g, to)

    def first_line(d):
        to = (place + d) % line * 2 + core
        return push(first.at[c], first.at[c], fz_s.at[d], fz_r.at[d], g, to)

    def first_pair(d):
        block = (place + d) % line * 2 + core
        return push(first.at[block], first.at[block], fx_s.at[d], fx_r.at[d], g, pair)

    def row_pair(block):
        at = block // 2
        return push(rows.at[block], rows.at[block], rx_s.at[at], rx_r.at[at], g, pair)

    def row_up(s):
        block = c - 2 * s
        return push(rows.at[block], rows.at[block], up_s.at[s], up_r.at[s], g, c + 2)

    def row_down(s):
        block = c + 2 * s
        return push(rows.at[block], rows.at[block], dn_s.at[s], dn_r.at[s], g, c - 2)

    def col_plane(d):
        return push(cols.at[:, g], cols.at[:, g], cp_s.at[d], cp_r.at[d], (g + d) % n_rows, c)

    def send_rows(s):
        @pl.when((place >= s) & (place + 1 < line))
        def _():
            row_up(s).start()

        @pl.when((place + s < line) & (place > 0))
        def _():
            row_down(s).start()

    def relay_rows(s):
        @pl.when(place > s)
        def _():
            row_up(s).wait_recv()
            row_pair(c - 2 * (s + 1)).start()

        @pl.when(place + s + 1 < line)
        def _():
            row_down(s).wait_recv()
            row_pair(c + 2 * (s + 1)).start()

        if s + 1 < line - 1:
            send_rows(s + 1)

    own = [
        pltpu.make_async_copy(first_in, first.at[c, g], own_sem.at[0]),
        pltpu.make_async_copy(row_in.at[g], plane_ref.at[g], own_sem.at[1]),
        pltpu.make_async_copy(col_in.at[c], cols.at[c, g], own_sem.at[2]),
    ]
    for copy in own:
        copy.start()
    for d in range(1, n_rows):
        first_plane(d).start()
    for d in range(1, n_rows):
        row_plane(d).start()
    for copy in own:
        copy.wait()
    for d in range(1, n_rows):
        first_plane(d).wait_recv()
    for d in range(1, line):
        first_line(d).start()
    first_pair(0).start()
    for d in range(1, n_cols):
        col_line(d).start()
    for d in range(1, n_rows):
        row_plane(d).wait_recv()
    height = turned_ref.shape[0]
    for n in range(height // P_SIZE):
        at = slice(n * P_SIZE, (n + 1) * P_SIZE)
        turned_ref[at, :] = plane_ref[:, :, at].reshape(-1, P_SIZE).T
    turned = pltpu.make_async_copy(turned_ref, rows.at[c], own_sem.at[3])
    turned.start()
    turned.wait()
    send_rows(0)
    row_pair(c).start()
    for d in range(1, line):
        first_line(d).wait_recv()
        first_pair(line - d).start()
    for d in range(line):
        first_pair(d).wait_recv()
    load = pltpu.make_async_copy(first, s0_ref, load_sem)
    load.start()
    load.wait()
    s0 = s0_ref[...].reshape(-1, P_SIZE)
    factor_start(s0, ridge_ref[...], a_ref, inv_ref)

    def col_gather():
        for d in range(1, n_cols):
            col_line(d).wait_recv()
        for d in range(1, n_rows):
            col_plane(d).start()

    def step(k, carry):
        factor_step(k, a_ref, lower_ref, inv_ref)

        @pl.when(k == 1)
        def _():
            relay_rows(0)
            col_gather()

        @pl.when(k == 3)
        def _():
            relay_rows(1)

        return carry

    lax.fori_loop(0, TILES, step, 0)
    factor_end(s0_ref[...].reshape(-1, P_SIZE), inv_ref, vh_ref, vl_ref)
    for d in range(1, n_rows):
        col_plane(d).wait_recv()
    load = pltpu.make_async_copy(cols, sc_ref, load_sem)
    load.start()
    load.wait()
    make_weights(g, c, s0_ref, sc_ref, vh_ref, vl_ref, lower_ref, inv_ref,
                 th_ref, tl_ref, strip_ref)
    for s in range(2, line - 1):
        relay_rows(s)
    for q in range(line):
        block = 2 * q + core
        row_pair(block).wait_recv()
    for d in range(1, n_rows):
        first_plane(d).wait_send()
        row_plane(d).wait_send()
        col_plane(d).wait_send()
    for d in range(1, n_cols):
        col_line(d).wait_send()
    for d in range(1, line):
        first_line(d).wait_send()
    for d in range(line):
        first_pair(d).wait_send()
        row_pair(2 * d + core).wait_send()
    for s in range(line - 1):
        @pl.when((place >= s) & (place + 1 < line))
        def _():
            row_up(s).wait_send()

        @pl.when((place + s < line) & (place > 0))
        def _():
            row_down(s).wait_send()


def gather(first_in, row_in, col_in, ridge0, n_rows, n_cols):
    per_dev = first_in.shape[0]
    total = per_dev * n_rows * n_cols
    height, width = row_in.shape[2], col_in.shape[2]
    line = n_cols // 2

    def gathered(width):
        return jax.ShapeDtypeStruct((n_cols, n_rows, per_dev, width), BF16)

    far = pl.BlockSpec(memory_space=pl.ANY)
    near = pl.BlockSpec(memory_space=pltpu.VMEM)
    counts = [n_rows, n_rows, n_cols, line, line, line, line, line, n_rows]
    sems = [pltpu.SemaphoreType.DMA((n,)) for n in counts for _ in range(2)]
    return pl.pallas_call(
        functools.partial(gather_kernel, n_rows, n_cols),
        out_shape=(
            jax.ShapeDtypeStruct((n_cols, height, n_rows * per_dev), BF16),
            gathered(width), gathered(P_SIZE),
            jax.ShapeDtypeStruct((total, width), BF16),
            jax.ShapeDtypeStruct((total, width), BF16),
            jax.ShapeDtypeStruct((B, width), F32),
        ),
        in_specs=[far, far, far, near],
        out_specs=[far, far, far, near, near, near],
        scratch_shapes=[
            pltpu.VMEM((P_SIZE, P_SIZE), F32),
            pltpu.VMEM((n_cols, n_rows, per_dev, P_SIZE), BF16),
            pltpu.VMEM((P_SIZE, P_SIZE), F32),
            pltpu.VMEM((P_SIZE, P_SIZE), F32),
            pltpu.VMEM((total, P_SIZE), BF16),
            pltpu.VMEM((total, P_SIZE), BF16),
            pltpu.VMEM((n_cols, n_rows, per_dev, width), BF16),
            pltpu.VMEM((n_rows, per_dev, height), BF16),
            pltpu.VMEM((height, n_rows * per_dev), BF16),
            pltpu.SemaphoreType.DMA((4,)),
            pltpu.SemaphoreType.DMA,
        ] + sems,
        compiler_params=pltpu.CompilerParams(
            vmem_limit_bytes=58 * MIB, collective_id=0, has_side_effects=True
        ),
        name="gather",
    )(first_in, row_in, col_in, ridge0)


def outer_kernel(n_rows, n_cols, ids, sr_ref, th_ref, tl_ref, strip_ref, ridge_ref, out_ref, t8_ref):
    i0 = pl.program_id(0)
    bm = sr_ref.shape[1]
    blocks = sr_ref.shape[0]
    width = th_ref.shape[1]
    tile_cols = width // B
    @pl.when(i0 == 0)
    def _():
        for n in range(width // 256):
            at = slice(n * 256, (n + 1) * 256)
            t8_ref[:, at] = (tl_ref[:, at].astype(F32) * LOW_SCALE).astype(F8)

    left = jnp.concatenate([sr_ref[q] for q in range(blocks)], axis=1)
    left8 = left.astype(F8)
    bn = min(256, width)
    for n in range(width // bn):
        at = slice(n * bn, (n + 1) * bn)
        low = dot(left8, t8_ref[:, at], (1, 0))
        acc = dot(left, th_ref[:, at], (1, 0)) + low * (1.0 / LOW_SCALE)
        for q in range(bn // B):
            j = n * (bn // B) + q
            out_ref[pl.ds(j, bm, stride=tile_cols), :] = acc[:, q * B : (q + 1) * B]

    row_id, col_id = ids[0], ids[1]

    @pl.when((i0 == 0) & (row_id < TILES))
    def _():
        for j in range(tile_cols):
            out_ref[pl.ds(j, B, stride=tile_cols), :] = strip_ref[:, j * B : (j + 1) * B]

    for u in range(bm // B):
        t = (i0 * (bm // B) + u) * n_rows + row_id

        @pl.when((t >= TILES) & (lax.rem(t, n_cols) == col_id))
        def _():
            at = pl.ds(u * B * tile_cols + lax.div(t, n_cols), B, stride=tile_cols)
            out_ref[at, :] += jnp.where(eye(B), ridge_ref[pl.ds(t, 1), :], 0.0)


def outer(ids, sr, th, tl, strip, ridge, n_rows, n_cols):
    blocks, height, deep = sr.shape
    total = blocks * deep
    width = th.shape[1]
    tile_cols = width // B
    bm = 512 if total <= 1024 else 256

    def whole(a):
        return pl.BlockSpec(a.shape, lambda i, ids: (0, 0), pipeline_mode=pl.Buffered(1))

    return pl.pallas_call(
        functools.partial(outer_kernel, n_rows, n_cols),
        out_shape=jax.ShapeDtypeStruct((height * tile_cols, B), F32),
        grid_spec=pltpu.PrefetchScalarGridSpec(
            num_scalar_prefetch=1,
            grid=(height // bm,),
            in_specs=[
                pl.BlockSpec((blocks, bm, deep), lambda i, ids: (0, i, 0)),
                whole(th), whole(tl), whole(strip), whole(ridge),
            ],
            out_specs=pl.BlockSpec((bm * tile_cols, B), lambda i, ids: (i, 0)),
            scratch_shapes=[pltpu.VMEM((total, width), F8)],
        ),
        compiler_params=pltpu.CompilerParams(vmem_limit_bytes=56 * MIB),
        name="outer",
    )(ids, sr, th, tl, strip, ridge)


def body(samples, ridge):
    row_id = lax.axis_index("gr")
    col_id = lax.axis_index("gc")
    n_rows = lax.axis_size("gr")
    n_cols = lax.axis_size("gc")
    per_dev, width = samples.shape
    tile_rows = width // (B * n_rows)
    tile_cols = width // (B * n_cols)
    row_in = samples.reshape(per_dev, tile_rows, n_rows, B).transpose(2, 0, 1, 3)
    col_in = samples.reshape(per_dev, tile_cols, n_cols, B).transpose(2, 0, 1, 3)
    rows_all, _, _, th, tl, strip = gather(
        samples[:, :P_SIZE],
        row_in.reshape(n_rows, per_dev, -1),
        col_in.reshape(n_cols, per_dev, -1),
        ridge[:P_SIZE].reshape(1, P_SIZE),
        n_rows,
        n_cols,
    )
    ids = jnp.stack([row_id, col_id]).astype(jnp.int32)
    result = outer(ids, rows_all, th, tl, strip, ridge.reshape(-1, B), n_rows, n_cols)
    return result.reshape(1, tile_rows, B, 1, tile_cols, B)


def solution(mesh):
    in_specs = (P(("gr", "gc"), None), P())
    out_specs = P("gr", None, None, "gc", None, None)
    return jax.shard_map(body, mesh=mesh, in_specs=in_specs, out_specs=out_specs, check_vma=False)
```
